128 devices in a mesh: band: 8 (over x, y_lo), domain: 16 (over y_hi, z, core).
Axes of the slice: x: 4, y: 4 (y_hi: 2, y_lo: 2; y = y_hi * 2 + y_lo), z: 4, core: 2. Of those that a mesh axis runs over, the one named last changes fastest.
Arguments:
- orbitals: float32 [96, 32, 24, 1024], P('domain', None, None, 'band'), may hold values from -6 to 6
- potential: float32 [96, 32, 24], P('domain'), may hold values from -3 to 0
Outputs:
- filtered: float32 [96, 32, 24, 1024], P('domain', None, None, 'band')
- margin: float32 [1024, 1024], P('band', 'domain')
The draws below stay inside these ranges and needn't reach their ends.
All inputs are finite; a program needn't handle non-finite values.
Results may differ from the reference program's by a relative error of at most 0.00005.
Values sent between devices are 32-bit elements; how exact they have to be, the bound alone decides.
No kernel may reach another device: no remote copies, remote signals or barrier semaphores. Data moves between devices by JAX's collectives and lax.ppermute only.
A program may use at most 192 MiB of HBM per device.

```python
import jax
import jax.numpy as jnp
from jax import lax

NORB = 1024
CY = 32
CZ = 24
DEG = 3
NX = 96
NGRID = 73728


def block_scale(stream_key, extent, shards, low, high):
    def one(dim, parts):
        steps = jax.random.uniform(jax.random.fold_in(jax.random.fold_in(stream_key, 6), dim), (parts,), jnp.float32, low / len(shards), high / len(shards))
        return jnp.repeat(jnp.exp(steps), extent[dim] // parts).reshape((-1,) + (1,) * (len(extent) - dim - 1))

    gain = one(*shards[0])
    for cut in shards[1:]:
        gain = gain * one(*cut)
    return gain


def scatter_about(stream_key, shape, width, bound, shards=(), held_as=jnp.bfloat16):
    factor_of = block_scale(stream_key, shape, shards, -0.22, 0.18) if shards else 1.0
    result = jax.random.normal(stream_key, shape, jnp.float32) * width * factor_of
    return jnp.minimum(jnp.maximum(result, -bound), bound).astype(held_as)


def setup_inputs(seed: int = 0) -> dict:
    keys = jax.random.split(jax.random.key(seed), 3)
    return {
        "orbitals": scatter_about(keys[0], (NX, CY, CZ, NORB), 1.0, 6.0, ((0, 16), (3, 8)), jnp.float32),
        "potential": jnp.clip(-3.0 + 3.0 * jax.random.uniform(keys[1], (NX, CY, CZ), jnp.float32) ** block_scale(keys[1], (NX, CY, CZ), ((0, 16),), -0.2, 0.2), -3.0, 0.0),
    }


coeffs = (-5369.0 / 1800.0, 12.0 / 7.0, -15.0 / 56.0, 10.0 / 189.0, -1.0 / 112.0, 2.0 / 1925.0, -1.0 / 16632.0)
bound_floor = 0.0
bound_cut = 2.0
bound_top = 11.0


def apply_ham(field, potential):
    total = 3.0 * coeffs[0] * field
    for step in range(1, 7):
        cycle = jnp.roll(field, step, 0) + jnp.roll(field, -step, 0)
        cycle = cycle + jnp.roll(field, step, 1) + jnp.roll(field, -step, 1)
        cycle = cycle + jnp.roll(field, step, 2) + jnp.roll(field, -step, 2)
        total = total + coeffs[step] * cycle
    return -0.5 * total + potential[..., None] * field


def reference(orbitals, potential):
    half_width = (bound_top - bound_cut) / 2.0
    center = (bound_top + bound_cut) / 2.0
    sigma = half_width / (bound_floor - center)
    gamma = 2.0 / sigma
    prior = orbitals
    current = (apply_ham(orbitals, potential) - center * orbitals) * (sigma / half_width)
    for index in range(2, DEG + 1):
        second = 1.0 / (gamma - sigma)
        nxt = (apply_ham(current, potential) - center * current) * (2.0 * second / half_width) - (sigma * second) * prior
        prior = current
        current = nxt
        sigma = second
    flat = current.reshape(-1, current.shape[-1])
    margin = lax.dot_general(flat, flat, (((0,), (0,)), ((), ())), precision=lax.Precision.HIGHEST, preferred_element_type=jnp.float32)
    return current, margin * (1.0 / NGRID)
```

```python
import jax
import jax.numpy as jnp
import numpy as np
from jax import lax
from jax.experimental import pallas as pl
from jax.experimental.pallas import tpu as pltpu
from jax.sharding import PartitionSpec as P

DEG = 3

coeffs = (
    -5369.0 / 1800.0,
    12.0 / 7.0,
    -15.0 / 56.0,
    10.0 / 189.0,
    -1.0 / 112.0,
    2.0 / 1925.0,
    -1.0 / 16632.0,
)
bound_floor = 0.0
bound_cut = 2.0
bound_top = 11.0
center = (bound_top + bound_cut) / 2.0

NX, NY, NZ = 96, 32, 24
PTS = NY * NZ
LT = PTS // 128
BANDS, DOMS = 8, 16
PL = NX // DOMS
NORB = 1024
OB = NORB // BANDS
OD = OB // DOMS
ROWS = PL * LT * OD
POT = PL * LT
POT_PAD = 40
GRID = NX * PTS
VMEM = 60 * 1024 * 1024


def steps():
    half_width = (bound_top - bound_cut) / 2.0
    sigma = half_width / (bound_floor - center)
    gamma = 2.0 / sigma
    out = [(sigma / half_width, 0.0)]
    for _ in range(2, DEG + 1):
        second = 1.0 / (gamma - sigma)
        out.append((2.0 * second / half_width, sigma * second))
        sigma = second
    return out


def plane_matrix():
    def ring(n):
        m = np.zeros((n, n))
        for k in range(1, 7):
            for i in range(n):
                m[i, (i + k) % n] += coeffs[k]
                m[i, (i - k) % n] += coeffs[k]
        return m

    m = np.kron(ring(NY), np.eye(NZ)) + np.kron(np.eye(NY), ring(NZ))
    m = -0.5 * (m + 3.0 * coeffs[0] * np.eye(PTS))
    hi = np.asarray(m, jnp.bfloat16)
    lo = np.asarray(m - hi.astype(np.float64), jnp.bfloat16)
    return hi, lo


def split(value):
    hi = value.astype(jnp.bfloat16)
    return hi, (value - hi.astype(jnp.float32)).astype(jnp.bfloat16)


def spread_kernel(cells, pot, out):
    for p in range(PL):
        flat = cells[p].T
        for j in range(LT):
            at = (p * LT + j) * OD
            out[:, at : at + OD, :] = flat[:, j * 128 : (j + 1) * 128].reshape(DOMS, OD, 128)
    row = jnp.concatenate([pot[...], jnp.zeros((POT_PAD - POT, 128), jnp.float32)], 0)
    out[:, ROWS:, :] = jnp.broadcast_to(row[None], (DOMS, POT_PAD, 128))


def filter_kernel(cells, high, low, out, other, left, prod):
    def keep(s, j, i, pair):
        value = jnp.concatenate(pair, 0)
        hi, lo = split(value)
        at = pl.ds(pl.multiple_of(s * (PL * OD), 16) + (i - 1) * OD, 2 * OD)
        left[at, j * 128 : (j + 1) * 128] = hi
        left[at, PTS + j * 128 : PTS + (j + 1) * 128] = lo

    @pl.loop(0, DOMS)
    def _(s):
        for j in range(LT):
            tiles = [cells[s, (i * LT + j) * OD : (i * LT + j + 1) * OD, :] for i in range(PL)]
            for i in range(1, PL, 2):
                keep(s, j, i, tiles[i - 1 : i + 1])

    def step(cur, prior, new, scale, back, last):
        for n in range(PTS // 256):
            cols = slice(n * 256, (n + 1) * 256)
            prod[:, cols] = (
                jnp.dot(left[:, :PTS], high[:, cols], preferred_element_type=jnp.float32)
                + jnp.dot(left[:, PTS:], high[:, cols], preferred_element_type=jnp.float32)
                + jnp.dot(left[:, :PTS], low[:, cols], preferred_element_type=jnp.float32)
            )

        @pl.loop(0, DOMS)
        def _(s):
            before = lax.rem(s + DOMS - 1, DOMS)
            after = lax.rem(s + 1, DOMS)
            for j in range(LT):
                at = [slice((i * LT + j) * OD, (i * LT + j + 1) * OD) for i in range(PL)]
                line = [cur[b, at[i], :] for b in (before, s, after) for i in range(PL)]
                fresh = []
                for i in range(PL):
                    mid = PL + i
                    pot = cells[s, ROWS + i * LT + j, :][None]
                    rows = pl.ds(pl.multiple_of(s * (PL * OD), 16) + i * OD, OD)
                    total = prod[rows, j * 128 : (j + 1) * 128] + (pot - center) * line[mid]
                    for k in range(1, 7):
                        total = total + (-0.5 * coeffs[k]) * (line[mid + k] + line[mid - k])
                    value = scale * total
                    if prior is not None:
                        value = value - back * prior[s, at[i], :]
                    fresh.append(value)
                for i in range(PL):
                    new[s, at[i], :] = fresh[i]
                    if not last and i % 2:
                        keep(s, j, i, fresh[i - 1 : i + 1])

    (a0, _), (a1, b1), (a2, b2) = steps()
    step(cells, None, other, a0, 0.0, False)
    step(other, cells, out, a1, b1, False)
    step(out, other, other, a2, b2, True)
    out[...] = other[...]


def gather_kernel(cells, out):
    for p in range(PL):
        for j in range(LT):
            at = (p * LT + j) * OD
            tile = cells[:, at : at + OD, :].reshape(OB, 128)
            out[p * PTS + j * 128 : p * PTS + (j + 1) * 128, :] = tile.T


def margin_kernel(cells, out):
    his, los = [], []
    for b in range(BANDS):
        hi, lo = split(cells[b])
        his.append(hi)
        los.append(lo)
    hi, lo = jnp.concatenate(his, 1), jnp.concatenate(los, 1)

    def dot(x, y):
        return lax.dot_general(x, y, (((0,), (0,)), ((), ())), preferred_element_type=jnp.float32)

    for b in range(0, BANDS, 2):
        cols = slice(b * OB, (b + 2) * OB)
        block = dot(hi, hi[:, cols]) + dot(lo, hi[:, cols]) + dot(hi, lo[:, cols])
        out[b] = block[:, :OB].reshape(DOMS, NORB // DOMS, OB)
        out[b + 1] = block[:, OB:].reshape(DOMS, NORB // DOMS, OB)


def sum_kernel(parts, out):
    total = parts[0]
    for i in range(1, BANDS * DOMS):
        total = total + parts[i]
    out[...] = (total * (1.0 / GRID)).T


def call(kernel, shape, *args, scratch=()):
    return pl.pallas_call(
        kernel,
        out_shape=jax.ShapeDtypeStruct(shape, jnp.float32),
        scratch_shapes=list(scratch),
        compiler_params=pltpu.CompilerParams(vmem_limit_bytes=VMEM),
    )(*args)


def local(orbitals, potential, high, low):
    cells = call(
        spread_kernel,
        (DOMS, ROWS + POT_PAD, 128),
        orbitals.reshape(PL, PTS, OB),
        potential.reshape(POT, 128),
    )
    cells = lax.all_to_all(cells, "domain", 0, 0, tiled=True)
    cells = call(
        filter_kernel,
        (DOMS, ROWS, 128),
        cells,
        high,
        low,
        scratch=[
            pltpu.VMEM((DOMS, ROWS, 128), jnp.float32),
            pltpu.VMEM((NX * OD, 2 * PTS), jnp.bfloat16),
            pltpu.VMEM((NX * OD, PTS), jnp.float32),
        ],
    )
    cells = lax.all_to_all(cells, "domain", 0, 0, tiled=True)
    flat = call(gather_kernel, (PL * PTS, OB), cells)
    points = lax.all_to_all(flat.reshape(BANDS, PL * PTS // BANDS, OB), "band", 0, 0, tiled=True)
    partial = call(margin_kernel, (BANDS, DOMS, NORB // DOMS, OB), points)
    partial = partial.reshape(BANDS * DOMS, NORB // DOMS, OB)
    partial = lax.all_to_all(partial, ("band", "domain"), 0, 0, tiled=True)
    margin = call(sum_kernel, (OB, NORB // DOMS), partial)
    return flat.reshape(PL, NY, NZ, OB), margin


def solution(mesh):
    grid, pot = P("domain", None, None, "band"), P("domain", None, None)
    high, low = plane_matrix()
    body = jax.shard_map(
        local,
        mesh=mesh,
        in_specs=(grid, pot, P(), P()),
        out_specs=(grid, P("band", "domain")),
        check_vma=False,
    )

    def run(orbitals, potential):
        return body(orbitals, potential, jnp.asarray(high), jnp.asarray(low))

    return run
```

```python
import jax
import jax.numpy as jnp
import numpy as np
from jax import lax
from jax.experimental import pallas as pl
from jax.experimental.pallas import tpu as pltpu
from jax.sharding import PartitionSpec as P

DEG = 3

coeffs = (
    -5369.0 / 1800.0,
    12.0 / 7.0,
    -15.0 / 56.0,
    10.0 / 189.0,
    -1.0 / 112.0,
    2.0 / 1925.0,
    -1.0 / 16632.0,
)
bound_floor = 0.0
bound_cut = 2.0
bound_top = 11.0
center = (bound_top + bound_cut) / 2.0

NX, NY, NZ = 96, 32, 24
PTS = NY * NZ
LT = PTS // 128
BANDS, DOMS = 8, 16
PL = NX // DOMS
NORB = 1024
OB = NORB // BANDS
OD = OB // DOMS
ROWS = PL * LT * OD
POT = PL * LT
POT_PAD = 40
TURNS = 2
GRID = NX * PTS
MIB = 1024 * 1024


def steps():
    half_width = (bound_top - bound_cut) / 2.0
    sigma = half_width / (bound_floor - center)
    gamma = 2.0 / sigma
    scales, backs = [sigma / half_width], [0.0]
    for _ in range(2, DEG + 1):
        second = 1.0 / (gamma - sigma)
        scales.append(2.0 * second / half_width)
        backs.append(sigma * second)
        sigma = second
    out = [(0.0, 1.0)]
    for i in range(1, DEG):
        out.append((backs[i] / (scales[i] * scales[i - 1]), float(np.prod(scales)) if i == DEG - 1 else 1.0))
    return out


def plane_matrix():
    def ring(n):
        m = np.zeros((n, n))
        for k in range(1, 7):
            for i in range(n):
                m[i, (i + k) % n] += coeffs[k]
                m[i, (i - k) % n] += coeffs[k]
        return m

    m = np.kron(ring(NY), np.eye(NZ)) + np.kron(np.eye(NY), ring(NZ))
    m = -0.5 * (m + 3.0 * coeffs[0] * np.eye(PTS))
    hi = np.asarray(m, jnp.bfloat16)
    lo = np.asarray(m - hi.astype(np.float64), jnp.bfloat16)
    return hi, lo


def split(value):
    hi = value.astype(jnp.bfloat16)
    return hi, (value - hi.astype(jnp.float32)).astype(jnp.bfloat16)


def spread_kernel(cells, pot, out):
    for p in range(PL):
        flat = cells[p].T
        for j in range(LT):
            at = (p * LT + j) * OD
            out[:, at : at + OD, :] = flat[:, j * 128 : (j + 1) * 128].reshape(DOMS, OD, 128)
    turned = jnp.concatenate([(pot[p] - center).T for p in range(PL)], 0)
    spot = lax.broadcasted_iota(jnp.int32, (NZ, PTS), 1)
    pick = (lax.rem(spot, NZ) == lax.broadcasted_iota(jnp.int32, (NZ, PTS), 0)).astype(jnp.float32)
    wide = jnp.dot(turned, pick, precision=lax.Precision.HIGHEST, preferred_element_type=jnp.float32)
    point = lax.broadcasted_iota(jnp.int32, (NY, PTS), 1)
    first = lax.broadcasted_iota(jnp.int32, (NY, PTS), 0) * NZ
    keep = (point >= first) & (point < first + NZ)
    for p in range(PL):
        row = jnp.sum(jnp.where(keep, wide[p * NY : (p + 1) * NY, :], 0.0), 0, keepdims=True)
        for j in range(LT):
            at = ROWS + p * LT + j
            out[:, at : at + 1, :] = jnp.broadcast_to(row[None, :, j * 128 : (j + 1) * 128], (DOMS, 1, 128))
    out[:, ROWS + POT :, :] = jnp.zeros((DOMS, POT_PAD - POT, 128), jnp.float32)


def filter_kernel(cells, high, low, out, one, two, left_a, left_b, prod_a, prod_b):
    group = DOMS // TURNS
    at = [[slice((i * LT + j) * OD, (i * LT + j + 1) * OD) for i in range(PL)] for j in range(LT)]

    def keep(left, s, i, j, pair):
        rows = slice((s * PL + i - 1) * OD, (s * PL + i + 1) * OD)
        hi, lo = split(jnp.concatenate(pair, 0))
        left[rows, j * 128 : (j + 1) * 128] = hi
        left[rows, PTS + j * 128 : PTS + (j + 1) * 128] = lo

    def planes(left, prod, turn):
        rows = slice(turn * group * PL * OD, (turn + 1) * group * PL * OD)
        for n in range(PTS // 256):
            cols = slice(n * 256, (n + 1) * 256)
            prod[rows, cols] = (
                jnp.dot(left[rows, :PTS], high[:, cols], preferred_element_type=jnp.float32)
                + jnp.dot(left[rows, PTS:], high[:, cols], preferred_element_type=jnp.float32)
                + jnp.dot(left[rows, :PTS], low[:, cols], preferred_element_type=jnp.float32)
            )

    def across(cur, prior, new, prod, left, back, scale, turn):
        for s in range(turn * group, (turn + 1) * group):
            for j in range(LT):
                line = [cur[b % DOMS, at[j][i], :] for b in (s - 1, s, s + 1) for i in range(PL)]
                fresh = []
                for i in range(PL):
                    mid = PL + i
                    row = (s * PL + i) * OD
                    pot = cells[s, ROWS + i * LT + j, :][None]
                    total = prod[row : row + OD, j * 128 : (j + 1) * 128] + pot * line[mid]
                    for k in range(1, 7):
                        total = total + (-0.5 * coeffs[k]) * (line[mid + k] + line[mid - k])
                    if prior is not None:
                        total = total - back * prior[s, at[j][i], :]
                    if scale != 1.0:
                        total = total * scale
                    fresh.append(total)
                for i in range(PL):
                    new[s, at[j][i], :] = fresh[i]
                    if left is not None and i % 2:
                        keep(left, s, i, j, fresh[i - 1 : i + 1])

    for turn in range(TURNS):
        for s in range(turn * group, (turn + 1) * group):
            for j in range(LT):
                for i in range(1, PL, 2):
                    keep(left_a, s, i, j, [cells[s, at[j][i - 1], :], cells[s, at[j][i], :]])
        planes(left_a, prod_a, turn)
    values, lefts, prods = [cells, one, two, out], [left_a, left_b, left_a, None], [prod_a, prod_b, prod_a]
    for i, (back, scale) in enumerate(steps()):
        for turn in range(TURNS):
            across(values[i], values[i - 1] if i else None, values[i + 1], prods[i], lefts[i + 1], back, scale, turn)
            if i < DEG - 1:
                planes(lefts[i + 1], prods[i + 1], turn)


def gather_kernel(cells, out):
    for p in range(PL):
        for j in range(LT):
            at = (p * LT + j) * OD
            tile = cells[:, at : at + OD, :].reshape(OB, 128)
            out[p * PTS + j * 128 : p * PTS + (j + 1) * 128, :] = tile.T


def margin_kernel(cells, mine, others, left_hi, left_lo, right_hi, right_lo):
    wide = 2 * OB
    nd = NORB // DOMS
    even = lax.rem(lax.axis_index("core"), 2) == 0
    for b in range(BANDS):
        cols = slice(b * OB, (b + 1) * OB)
        right_hi[:, cols], right_lo[:, cols] = split(cells[b])
        left_hi[cols, :], left_lo[cols, :] = split(cells[b].T)

    def put(block, rows, cols):
        for c in range(2):
            for r in range(2):
                low = block[2 * r * nd : (2 * r + 1) * nd, c * OB : (c + 1) * OB]
                high = block[(2 * r + 1) * nd : (2 * r + 2) * nd, c * OB : (c + 1) * OB]
                mine[2 * cols + c, 2 * rows + r] = jnp.where(even, low, high)
                others[2 * cols + c, 2 * rows + r] = jnp.where(even, high, low)

    for i in range(NORB // wide):
        for j in range(i + 1):
            rows, cols = slice(i * wide, (i + 1) * wide), slice(j * wide, (j + 1) * wide)
            block = (
                jnp.dot(left_hi[rows, :], right_hi[:, cols], preferred_element_type=jnp.float32)
                + jnp.dot(left_lo[rows, :], right_hi[:, cols], preferred_element_type=jnp.float32)
                + jnp.dot(left_hi[rows, :], right_lo[:, cols], preferred_element_type=jnp.float32)
            )
            put(block, i, j)
            if i != j:
                put(block.T, j, i)


def sum_kernel(parts, out):
    total = parts[0]
    for i in range(1, BANDS * DOMS // 2):
        total = total + parts[i]
    out[...] = total * (1.0 / GRID)


def call(kernel, shape, *args, scratch=(), limit=16):
    shapes = shape if isinstance(shape, list) else [shape]
    out = [jax.ShapeDtypeStruct(s, jnp.float32) for s in shapes]
    return pl.pallas_call(
        kernel,
        out_shape=out if isinstance(shape, list) else out[0],
        scratch_shapes=list(scratch),
        compiler_params=pltpu.CompilerParams(vmem_limit_bytes=limit * MIB),
    )(*args)


BAND = ("x", "y_lo")
DOMAIN = ("y_hi", "z", "core")
CHIPS = ("x", "y_lo", "y_hi", "z")


def local(orbitals, potential, high, low):
    cells = call(
        spread_kernel,
        (DOMS, ROWS + POT_PAD, 128),
        orbitals.reshape(PL, PTS, OB),
        potential.transpose(0, 2, 1),
    )
    cells = lax.all_to_all(cells, DOMAIN, 0, 0, tiled=True)
    cells = call(
        filter_kernel,
        (DOMS, ROWS, 128),
        cells,
        high,
        low,
        scratch=[pltpu.VMEM((DOMS, ROWS, 128), jnp.float32)] * 2
        + [pltpu.VMEM((NX * OD, 2 * PTS), jnp.bfloat16)] * 2
        + [pltpu.VMEM((NX * OD, PTS), jnp.float32)] * 2,
        limit=32,
    )
    cells = lax.all_to_all(cells, DOMAIN, 0, 0, tiled=True)
    flat = call(gather_kernel, (PL * PTS, OB), cells)
    count = PL * PTS // BANDS
    points = lax.all_to_all(flat.reshape(BANDS, count, OB), BAND, 0, 0, tiled=True)
    shape = (BANDS, DOMS // 2, NORB // DOMS, OB)
    mine, others = call(
        margin_kernel,
        [shape, shape],
        points,
        scratch=[pltpu.VMEM((NORB, count), jnp.bfloat16)] * 2 + [pltpu.VMEM((count, NORB), jnp.bfloat16)] * 2,
        limit=24,
    )
    partial = mine + lax.ppermute(others, "core", [(0, 1), (1, 0)])
    partial = partial.reshape(BANDS * DOMS // 2, NORB // DOMS, OB)
    partial = lax.all_to_all(partial, CHIPS, 0, 0, tiled=True)
    margin = call(sum_kernel, (NORB // DOMS, OB), partial)
    return flat.reshape(PL, NY, NZ, OB), margin.T


def solution(mesh):
    mesh = jax.sharding.Mesh(mesh.devices.reshape(4, 2, 2, 4, 2), BAND + DOMAIN)
    grid, pot = P(DOMAIN, None, None, BAND), P(DOMAIN, None, None)
    high, low = plane_matrix()
    body = jax.shard_map(
        local,
        mesh=mesh,
        in_specs=(grid, pot, P(), P()),
        out_specs=(grid, P(BAND, DOMAIN)),
        check_vma=False,
    )

    def run(orbitals, potential):
        return body(orbitals, potential, jnp.asarray(high), jnp.asarray(low))

    return run
```

```python
import jax
import jax.numpy as jnp
import numpy as np
from jax import lax
from jax.experimental import pallas as pl
from jax.experimental.pallas import tpu as pltpu
from jax.sharding import PartitionSpec as P

DEG = 3

coeffs = (
    -5369.0 / 1800.0,
    12.0 / 7.0,
    -15.0 / 56.0,
    10.0 / 189.0,
    -1.0 / 112.0,
    2.0 / 1925.0,
    -1.0 / 16632.0,
)
bound_floor = 0.0
bound_cut = 2.0
bound_top = 11.0
center = (bound_top + bound_cut) / 2.0

NX, NY, NZ = 96, 32, 24
PTS = NY * NZ
LT = PTS // 128
BANDS, DOMS = 8, 16
PL = NX // DOMS
NORB = 1024
OB = NORB // BANDS
OD = OB // DOMS
ROWS = PL * LT * OD
POT = PL * LT
POT_PAD = 40
TURNS = 2
GRID = NX * PTS
MIB = 1024 * 1024


def steps():
    half_width = (bound_top - bound_cut) / 2.0
    sigma = half_width / (bound_floor - center)
    gamma = 2.0 / sigma
    scales, backs = [sigma / half_width], [0.0]
    for _ in range(2, DEG + 1):
        second = 1.0 / (gamma - sigma)
        scales.append(2.0 * second / half_width)
        backs.append(sigma * second)
        sigma = second
    out = [(0.0, 1.0)]
    for i in range(1, DEG):
        out.append((backs[i] / (scales[i] * scales[i - 1]), float(np.prod(scales)) if i == DEG - 1 else 1.0))
    return out


def plane_matrix():
    def ring(n):
        m = np.zeros((n, n))
        for k in range(1, 7):
            for i in range(n):
                m[i, (i + k) % n] += coeffs[k]
                m[i, (i - k) % n] += coeffs[k]
        return m

    m = np.kron(ring(NY), np.eye(NZ)) + np.kron(np.eye(NY), ring(NZ))
    m = -0.5 * (m + 3.0 * coeffs[0] * np.eye(PTS))
    hi = np.asarray(m, jnp.bfloat16)
    lo = np.asarray(m - hi.astype(np.float64), jnp.bfloat16)
    return hi, lo


def split(value):
    hi = value.astype(jnp.bfloat16)
    return hi, (value - hi.astype(jnp.float32)).astype(jnp.bfloat16)


def spread_kernel(cells, out):
    flat = cells[0].T
    for j in range(LT):
        out[:, j * OD : (j + 1) * OD, :] = flat[:, j * 128 : (j + 1) * 128].reshape(DOMS, OD, 128)


def potential_kernel(pot, out):
    turned = jnp.concatenate([(pot[p] - center).T for p in range(PL)], 0)
    spot = lax.broadcasted_iota(jnp.int32, (NZ, PTS), 1)
    pick = (lax.rem(spot, NZ) == lax.broadcasted_iota(jnp.int32, (NZ, PTS), 0)).astype(jnp.float32)
    wide = jnp.dot(turned, pick, precision=lax.Precision.HIGHEST, preferred_element_type=jnp.float32)
    point = lax.broadcasted_iota(jnp.int32, (NY, PTS), 1)
    first = lax.broadcasted_iota(jnp.int32, (NY, PTS), 0) * NZ
    keep = (point >= first) & (point < first + NZ)
    for p in range(PL):
        row = jnp.sum(jnp.where(keep, wide[p * NY : (p + 1) * NY, :], 0.0), 0, keepdims=True)
        for j in range(LT):
            at = p * LT + j
            out[at : at + 1, :] = row[:, j * 128 : (j + 1) * 128]
    out[POT:, :] = jnp.zeros((POT_PAD - POT, 128), jnp.float32)


def filter_kernel(cells, field, high, low, out, one, two, left_a, left_b, prod_a, prod_b):
    group = DOMS // TURNS
    at = [[slice((i * LT + j) * OD, (i * LT + j + 1) * OD) for i in range(PL)] for j in range(LT)]

    def keep(left, s, i, j, pair):
        rows = slice((s * PL + i - 1) * OD, (s * PL + i + 1) * OD)
        hi, lo = split(jnp.concatenate(pair, 0))
        left[rows, j * 128 : (j + 1) * 128] = hi
        left[rows, PTS + j * 128 : PTS + (j + 1) * 128] = lo

    def planes(left, prod, turn):
        rows = slice(turn * group * PL * OD, (turn + 1) * group * PL * OD)
        for n in range(PTS // 256):
            cols = slice(n * 256, (n + 1) * 256)
            prod[rows, cols] = (
                jnp.dot(left[rows, :PTS], high[:, cols], preferred_element_type=jnp.float32)
                + jnp.dot(left[rows, PTS:], high[:, cols], preferred_element_type=jnp.float32)
                + jnp.dot(left[rows, :PTS], low[:, cols], preferred_element_type=jnp.float32)
            )

    def across(cur, prior, new, prod, left, back, scale, turn):
        for s in range(turn * group, (turn + 1) * group):
            for j in range(LT):
                line = [cur[b % DOMS, at[j][i], :] for b in (s - 1, s, s + 1) for i in range(PL)]
                fresh = []
                for i in range(PL):
                    mid = PL + i
                    row = (s * PL + i) * OD
                    pot = field[s, i * LT + j, :][None]
                    total = prod[row : row + OD, j * 128 : (j + 1) * 128] + pot * line[mid]
                    for k in range(1, 7):
                        total = total + (-0.5 * coeffs[k]) * (line[mid + k] + line[mid - k])
                    if prior is not None:
                        total = total - back * prior[s, at[j][i], :]
                    if scale != 1.0:
                        total = total * scale
                    fresh.append(total)
                for i in range(PL):
                    new[s, at[j][i], :] = fresh[i]
                    if left is not None and i % 2:
                        keep(left, s, i, j, fresh[i - 1 : i + 1])

    for turn in range(TURNS):
        for s in range(turn * group, (turn + 1) * group):
            for j in range(LT):
                for i in range(1, PL, 2):
                    keep(left_a, s, i, j, [cells[s, at[j][i - 1], :], cells[s, at[j][i], :]])
        planes(left_a, prod_a, turn)
    values, lefts, prods = [cells, one, two, out], [left_a, left_b, left_a, None], [prod_a, prod_b, prod_a]
    for i, (back, scale) in enumerate(steps()):
        for turn in range(TURNS):
            across(values[i], values[i - 1] if i else None, values[i + 1], prods[i], lefts[i + 1], back, scale, turn)
            if i < DEG - 1:
                planes(lefts[i + 1], prods[i + 1], turn)


def gather_kernel(cells, out):
    start = pl.multiple_of(pl.program_id(0) * (LT * OD), LT * OD)
    for j in range(LT):
        tile = cells[:, pl.ds(start + j * OD, OD), :].reshape(OB, 128)
        out[j * 128 : (j + 1) * 128, :] = tile.T


def margin_kernel(cells, mine, others, left_hi, left_lo, right_hi, right_lo):
    wide = 2 * OB
    nd = NORB // DOMS
    even = lax.rem(lax.axis_index("core"), 2) == 0
    for b in range(BANDS):
        cols = slice(b * OB, (b + 1) * OB)
        right_hi[:, cols], right_lo[:, cols] = split(cells[b])
        left_hi[cols, :], left_lo[cols, :] = split(cells[b].T)

    def put(block, rows, cols):
        for c in range(2):
            for r in range(2):
                low = block[2 * r * nd : (2 * r + 1) * nd, c * OB : (c + 1) * OB]
                high = block[(2 * r + 1) * nd : (2 * r + 2) * nd, c * OB : (c + 1) * OB]
                mine[2 * cols + c, 2 * rows + r] = jnp.where(even, low, high)
                others[2 * cols + c, 2 * rows + r] = jnp.where(even, high, low)

    for i in range(NORB // wide):
        for j in range(i + 1):
            rows, cols = slice(i * wide, (i + 1) * wide), slice(j * wide, (j + 1) * wide)
            block = (
                jnp.dot(left_hi[rows, :], right_hi[:, cols], preferred_element_type=jnp.float32)
                + jnp.dot(left_lo[rows, :], right_hi[:, cols], preferred_element_type=jnp.float32)
                + jnp.dot(left_hi[rows, :], right_lo[:, cols], preferred_element_type=jnp.float32)
            )
            put(block, i, j)
            if i != j:
                put(block.T, j, i)


def sum_kernel(parts, out):
    total = parts[0]
    for i in range(1, BANDS * DOMS // 2):
        total = total + parts[i]
    out[...] = total * (1.0 / GRID)


def call(kernel, shape, *args, scratch=(), limit=16):
    shapes = shape if isinstance(shape, list) else [shape]
    out = [jax.ShapeDtypeStruct(s, jnp.float32) for s in shapes]
    return pl.pallas_call(
        kernel,
        out_shape=out if isinstance(shape, list) else out[0],
        scratch_shapes=list(scratch),
        compiler_params=pltpu.CompilerParams(vmem_limit_bytes=limit * MIB),
    )(*args)


BAND = ("x", "y_lo")
DOMAIN = ("y_hi", "z", "core")
CHIPS = ("x", "y_lo", "y_hi", "z")


def local(orbitals, potential, high, low):
    cells = pl.pallas_call(
        spread_kernel,
        grid=(PL,),
        out_shape=jax.ShapeDtypeStruct((DOMS, ROWS, 128), jnp.float32),
        in_specs=[pl.BlockSpec((1, PTS, OB), lambda p: (p, 0, 0))],
        out_specs=pl.BlockSpec((DOMS, LT * OD, 128), lambda p: (0, p, 0)),
        compiler_params=pltpu.CompilerParams(vmem_limit_bytes=60 * MIB),
    )(orbitals.reshape(PL, PTS, OB))
    field = call(potential_kernel, (POT_PAD, 128), potential.transpose(0, 2, 1))
    field = lax.all_gather(field, DOMAIN)
    cells = lax.all_to_all(cells, DOMAIN, 0, 0, tiled=True)
    cells = pl.pallas_call(
        filter_kernel,
        out_shape=jax.ShapeDtypeStruct((DOMS, ROWS, 128), jnp.float32),
        scratch_shapes=[pltpu.VMEM((DOMS, ROWS, 128), jnp.float32)] * 2
        + [pltpu.VMEM((NX * OD, 2 * PTS), jnp.bfloat16)] * 2
        + [pltpu.VMEM((NX * OD, PTS), jnp.float32)] * 2,
        compiler_params=pltpu.CompilerParams(vmem_limit_bytes=48 * MIB),
    )(cells, field, high, low)
    cells = lax.all_to_all(cells, DOMAIN, 0, 0, tiled=True)
    flat = pl.pallas_call(
        gather_kernel,
        grid=(PL,),
        out_shape=jax.ShapeDtypeStruct((PL * PTS, OB), jnp.float32),
        in_specs=[pl.BlockSpec(memory_space=pltpu.VMEM)],
        out_specs=pl.BlockSpec((PTS, OB), lambda p: (p, 0)),
        compiler_params=pltpu.CompilerParams(vmem_limit_bytes=16 * MIB),
    )(cells)
    count = PL * PTS // BANDS
    points = lax.all_to_all(flat.reshape(BANDS, count, OB), BAND, 0, 0, tiled=True)
    shape = (BANDS, DOMS // 2, NORB // DOMS, OB)
    mine, others = call(
        margin_kernel,
        [shape, shape],
        points,
        scratch=[pltpu.VMEM((NORB, count), jnp.bfloat16)] * 2 + [pltpu.VMEM((count, NORB), jnp.bfloat16)] * 2,
        limit=24,
    )
    partial = mine + lax.ppermute(others, "core", [(0, 1), (1, 0)])
    partial = partial.reshape(BANDS * DOMS // 2, NORB // DOMS, OB)
    partial = lax.all_to_all(partial, CHIPS, 0, 0, tiled=True)
    margin = call(sum_kernel, (NORB // DOMS, OB), partial)
    return flat.reshape(PL, NY, NZ, OB), margin.T


def solution(mesh):
    mesh = jax.sharding.Mesh(mesh.devices.reshape(4, 2, 2, 4, 2), BAND + DOMAIN)
    grid, pot = P(DOMAIN, None, None, BAND), P(DOMAIN, None, None)
    high, low = plane_matrix()
    body = jax.shard_map(
        local,
        mesh=mesh,
        in_specs=(grid, pot, P(), P()),
        out_specs=(grid, P(BAND, DOMAIN)),
        check_vma=False,
    )

    def run(orbitals, potential):
        return body(orbitals, potential, jnp.asarray(high), jnp.asarray(low))

    return run
```

```python
import jax
import jax.numpy as jnp
import numpy as np
from jax import lax
from jax.experimental import pallas as pl
from jax.experimental.pallas import tpu as pltpu
from jax.sharding import PartitionSpec as P

DEG = 3

coeffs = (
    -5369.0 / 1800.0,
    12.0 / 7.0,
    -15.0 / 56.0,
    10.0 / 189.0,
    -1.0 / 112.0,
    2.0 / 1925.0,
    -1.0 / 16632.0,
)
bound_floor = 0.0
bound_cut = 2.0
bound_top = 11.0
center = (bound_top + bound_cut) / 2.0

NX, NY, NZ = 96, 32, 24
PTS = NY * NZ
LT = PTS // 128
BANDS, DOMS = 8, 16
PL = NX // DOMS
NORB = 1024
OB = NORB // BANDS
OD = OB // DOMS
ROWS = PL * LT * OD
POT = PL * LT
POT_PAD = 40
TURNS = 2
GRID = NX * PTS
MIB = 1024 * 1024


STRETCH = 35.0 / 16.0
along = [-0.5 * STRETCH * c for c in coeffs]


def steps():
    half_width = (bound_top - bound_cut) / 2.0
    sigma = half_width / (bound_floor - center)
    gamma = 2.0 / sigma
    scales, backs = [sigma / half_width / STRETCH], [0.0]
    for _ in range(2, DEG + 1):
        second = 1.0 / (gamma - sigma)
        scales.append(2.0 * second / half_width / STRETCH)
        backs.append(sigma * second)
        sigma = second
    out = [(0.0, 1.0)]
    for i in range(1, DEG):
        out.append((backs[i] / (scales[i] * scales[i - 1]), float(np.prod(scales)) if i == DEG - 1 else 1.0))
    return out


def plane_matrix():
    def ring(n):
        m = np.zeros((n, n))
        for k in range(1, 7):
            for i in range(n):
                m[i, (i + k) % n] += along[k]
                m[i, (i - k) % n] += along[k]
        return m

    return np.asarray(np.kron(ring(NY), np.eye(NZ)) + np.kron(np.eye(NY), ring(NZ)), jnp.bfloat16)


def split(value):
    hi = value.astype(jnp.bfloat16)
    return hi, (value - hi.astype(jnp.float32)).astype(jnp.bfloat16)


def spread_kernel(cells, pot, out):
    for p in range(PL):
        flat = cells[p].T
        for j in range(LT):
            at = (p * LT + j) * OD
            out[:, at : at + OD, :] = flat[:, j * 128 : (j + 1) * 128].reshape(DOMS, OD, 128)
    turned = jnp.concatenate([(STRETCH * (pot[p] - center) + 3.0 * along[0]).T for p in range(PL)], 0)
    spot = lax.broadcasted_iota(jnp.int32, (NZ, PTS), 1)
    pick = (lax.rem(spot, NZ) == lax.broadcasted_iota(jnp.int32, (NZ, PTS), 0)).astype(jnp.float32)
    wide = jnp.dot(turned, pick, precision=lax.Precision.HIGHEST, preferred_element_type=jnp.float32)
    point = lax.broadcasted_iota(jnp.int32, (NY, PTS), 1)
    first = lax.broadcasted_iota(jnp.int32, (NY, PTS), 0) * NZ
    keep = (point >= first) & (point < first + NZ)
    for p in range(PL):
        row = jnp.sum(jnp.where(keep, wide[p * NY : (p + 1) * NY, :], 0.0), 0, keepdims=True)
        for j in range(LT):
            at = ROWS + p * LT + j
            out[:, at : at + 1, :] = jnp.broadcast_to(row[None, :, j * 128 : (j + 1) * 128], (DOMS, 1, 128))
    out[:, ROWS + POT :, :] = jnp.zeros((DOMS, POT_PAD - POT, 128), jnp.float32)


def filter_kernel(cells, ring, out, one, two, left_a, left_b, prod_a, prod_b):
    group = DOMS // TURNS
    at = [[slice((i * LT + j) * OD, (i * LT + j + 1) * OD) for i in range(PL)] for j in range(LT)]

    def keep(left, s, i, j, pair):
        rows = slice((s * PL + i - 1) * OD, (s * PL + i + 1) * OD)
        hi, lo = split(jnp.concatenate(pair, 0))
        left[rows, j * 128 : (j + 1) * 128] = hi
        left[rows, PTS + j * 128 : PTS + (j + 1) * 128] = lo

    def planes(left, prod, turn):
        rows = slice(turn * group * PL * OD, (turn + 1) * group * PL * OD)
        for n in range(PTS // 256):
            cols = slice(n * 256, (n + 1) * 256)
            prod[rows, cols] = (
                jnp.dot(left[rows, :PTS], ring[:, cols], preferred_element_type=jnp.float32)
                + jnp.dot(left[rows, PTS:], ring[:, cols], preferred_element_type=jnp.float32)
            )

    def across(cur, prior, new, prod, left, back, scale, turn):
        for s in range(turn * group, (turn + 1) * group):
            for j in range(LT):
                line = [cur[b % DOMS, at[j][i], :] for b in (s - 1, s, s + 1) for i in range(PL)]
                fresh = []
                for i in range(PL):
                    mid = PL + i
                    row = (s * PL + i) * OD
                    pot = cells[s, ROWS + i * LT + j, :][None]
                    total = prod[row : row + OD, j * 128 : (j + 1) * 128] + pot * line[mid]
                    for k in range(1, 7):
                        total = total + along[k] * (line[mid + k] + line[mid - k])
                    if prior is not None:
                        total = total - back * prior[s, at[j][i], :]
                    if scale != 1.0:
                        total = total * scale
                    fresh.append(total)
                for i in range(PL):
                    new[s, at[j][i], :] = fresh[i]
                    if left is not None and i % 2:
                        keep(left, s, i, j, fresh[i - 1 : i + 1])

    for turn in range(TURNS):
        for s in range(turn * group, (turn + 1) * group):
            for j in range(LT):
                for i in range(1, PL, 2):
                    keep(left_a, s, i, j, [cells[s, at[j][i - 1], :], cells[s, at[j][i], :]])
        planes(left_a, prod_a, turn)
    values, lefts, prods = [cells, one, two, out], [left_a, left_b, left_a, None], [prod_a, prod_b, prod_a]
    for i, (back, scale) in enumerate(steps()):
        for turn in range(TURNS):
            across(values[i], values[i - 1] if i else None, values[i + 1], prods[i], lefts[i + 1], back, scale, turn)
            if i < DEG - 1:
                planes(lefts[i + 1], prods[i + 1], turn)


def gather_kernel(cells, out):
    for p in range(PL):
        for j in range(LT):
            at = (p * LT + j) * OD
            tile = cells[:, at : at + OD, :].reshape(OB, 128)
            out[p * PTS + j * 128 : p * PTS + (j + 1) * 128, :] = tile.T


def margin_blocks(parts, mine, others, pairs):
    left_hi, left_lo, right_hi, right_lo = parts
    wide = 2 * OB
    nd = NORB // DOMS
    even = lax.rem(lax.axis_index("core"), 2) == 0

    def put(block, i, j):
        for c in range(2):
            for r in range(2):
                first = block[2 * r * nd : (2 * r + 1) * nd, c * OB : (c + 1) * OB]
                second = block[(2 * r + 1) * nd : (2 * r + 2) * nd, c * OB : (c + 1) * OB]
                at = (j // 2, 2 * (j % 2) + c, 2 * (i % 2) + r)
                mine[at] = jnp.where(even, first, second)
                others[at] = jnp.where(even, second, first)

    for i, j in pairs:
        rows, cols = slice(i * wide, (i + 1) * wide), slice(j * wide, (j + 1) * wide)
        block = (
            jnp.dot(left_hi[rows, :], right_hi[:, cols], preferred_element_type=jnp.float32)
            + jnp.dot(left_lo[rows, :], right_hi[:, cols], preferred_element_type=jnp.float32)
            + jnp.dot(left_hi[rows, :], right_lo[:, cols], preferred_element_type=jnp.float32)
        )
        put(block, i, j)
        if i != j:
            put(block.T, j, i)


def far_kernel(cells, mine, others, left_hi, left_lo, right_hi, right_lo):
    for b in range(BANDS):
        cols = slice(b * OB, (b + 1) * OB)
        right_hi[:, cols], right_lo[:, cols] = split(cells[b])
        left_hi[cols, :], left_lo[cols, :] = split(cells[b].T)
    margin_blocks((left_hi, left_lo, right_hi, right_lo), mine, others, [(2, 0), (3, 0), (2, 1), (3, 1)])


def near_kernel(left_hi, left_lo, right_hi, right_lo, mine, others):
    parts = (left_hi, left_lo, right_hi, right_lo)
    margin_blocks(parts, mine, others, [(0, 0), (1, 0), (1, 1), (2, 2), (3, 2), (3, 3)])


def join_kernel(far, far_other, near, near_other, out):
    for h in range(2):
        here, there = slice(4 * h, 4 * h + 4), slice(4 - 4 * h, 8 - 4 * h)
        out[here, there] = far[h] + far_other[h]
        out[here, here] = near[h] + near_other[h]


def sum_kernel(parts, out):
    total = parts[0]
    for i in range(1, BANDS * DOMS // 2):
        total = total + parts[i]
    out[...] = total * (1.0 / GRID)


def call(kernel, shape, *args, scratch=(), limit=16):
    shapes = shape if isinstance(shape, list) else [shape]
    out = [jax.ShapeDtypeStruct(s, jnp.float32) for s in shapes]
    return pl.pallas_call(
        kernel,
        out_shape=out if isinstance(shape, list) else out[0],
        scratch_shapes=list(scratch),
        compiler_params=pltpu.CompilerParams(vmem_limit_bytes=limit * MIB),
    )(*args)


BAND = ("x", "y_lo")
DOMAIN = ("y_hi", "z", "core")
CHIPS = ("x", "y_lo", "y_hi", "z")


def local(orbitals, potential, ring):
    cells = call(
        spread_kernel,
        (DOMS, ROWS + POT_PAD, 128),
        orbitals.reshape(PL, PTS, OB),
        potential.transpose(0, 2, 1),
    )
    cells = lax.all_to_all(cells, DOMAIN, 0, 0, tiled=True)
    cells = call(
        filter_kernel,
        (DOMS, ROWS, 128),
        cells,
        ring,
        scratch=[pltpu.VMEM((DOMS, ROWS, 128), jnp.float32)] * 2
        + [pltpu.VMEM((NX * OD, 2 * PTS), jnp.bfloat16)] * 2
        + [pltpu.VMEM((NX * OD, PTS), jnp.float32)] * 2,
        limit=32,
    )
    cells = lax.all_to_all(cells, DOMAIN, 0, 0, tiled=True)
    flat = call(gather_kernel, (PL * PTS, OB), cells)
    count = PL * PTS // BANDS
    points = lax.all_to_all(flat.reshape(BANDS, count, OB), BAND, 0, 0, tiled=True)
    shape = (2, BANDS // 2, DOMS // 4, NORB // DOMS, OB)
    half = (jax.ShapeDtypeStruct(shape, jnp.float32),) * 2
    parts = (jax.ShapeDtypeStruct((NORB, count), jnp.bfloat16),) * 2
    parts += (jax.ShapeDtypeStruct((count, NORB), jnp.bfloat16),) * 2
    limits = pltpu.CompilerParams(vmem_limit_bytes=16 * MIB)
    far, far_other, *parts = pl.pallas_call(far_kernel, out_shape=half + parts, compiler_params=limits)(points)
    far_other = lax.ppermute(far_other, "core", [(0, 1), (1, 0)])
    near, near_other = pl.pallas_call(near_kernel, out_shape=half, compiler_params=limits)(*parts)
    near_other = lax.ppermute(near_other, "core", [(0, 1), (1, 0)])
    partial = call(join_kernel, (BANDS, DOMS // 2, NORB // DOMS, OB), far, far_other, near, near_other)
    partial = partial.reshape(BANDS * DOMS // 2, NORB // DOMS, OB)
    partial = lax.all_to_all(partial, CHIPS, 0, 0, tiled=True)
    margin = call(sum_kernel, (NORB // DOMS, OB), partial)
    return flat.reshape(PL, NY, NZ, OB), margin.T


def solution(mesh):
    mesh = jax.sharding.Mesh(mesh.devices.reshape(4, 2, 2, 4, 2), BAND + DOMAIN)
    grid, pot = P(DOMAIN, None, None, BAND), P(DOMAIN, None, None)
    ring = plane_matrix()
    body = jax.shard_map(
        local,
        mesh=mesh,
        in_specs=(grid, pot, P()),
        out_specs=(grid, P(BAND, DOMAIN)),
        check_vma=False,
    )

    def run(orbitals, potential):
        return body(orbitals, potential, jnp.asarray(ring))

    return run
```

```python
import jax
import jax.numpy as jnp
import numpy as np
from jax import lax
from jax.experimental import pallas as pl
from jax.experimental.pallas import tpu as pltpu
from jax.sharding import PartitionSpec as P

DEG = 3

coeffs = (
    -5369.0 / 1800.0,
    12.0 / 7.0,
    -15.0 / 56.0,
    10.0 / 189.0,
    -1.0 / 112.0,
    2.0 / 1925.0,
    -1.0 / 16632.0,
)
bound_floor = 0.0
bound_cut = 2.0
bound_top = 11.0
center = (bound_top + bound_cut) / 2.0

NX, NY, NZ = 96, 32, 24
PTS = NY * NZ
LT = PTS // 128
BANDS, DOMS = 8, 16
PL = NX // DOMS
NORB = 1024
OB = NORB // BANDS
OD = OB // DOMS
ROWS = PL * LT * OD
POT = PL * LT
POT_PAD = 40
TURNS = 2
GRID = NX * PTS
MIB = 1024 * 1024


STRETCH = 35.0 / 16.0
along = [-0.5 * STRETCH * c for c in coeffs]


def steps():
    half_width = (bound_top - bound_cut) / 2.0
    sigma = half_width / (bound_floor - center)
    gamma = 2.0 / sigma
    scales, backs = [sigma / half_width / STRETCH], [0.0]
    for _ in range(2, DEG + 1):
        second = 1.0 / (gamma - sigma)
        scales.append(2.0 * second / half_width / STRETCH)
        backs.append(sigma * second)
        sigma = second
    out = [(0.0, 1.0)]
    for i in range(1, DEG):
        out.append((backs[i] / (scales[i] * scales[i - 1]), float(np.prod(scales)) if i == DEG - 1 else 1.0))
    return out


def plane_matrix():
    def ring(n):
        m = np.zeros((n, n))
        for k in range(1, 7):
            for i in range(n):
                m[i, (i + k) % n] += along[k]
                m[i, (i - k) % n] += along[k]
        return m

    return np.asarray(np.kron(ring(NY), np.eye(NZ)) + np.kron(np.eye(NY), ring(NZ)), jnp.bfloat16)


def split(value):
    hi = value.astype(jnp.bfloat16)
    return hi, (value - hi.astype(jnp.float32)).astype(jnp.bfloat16)


def spread_kernel(cells, pot, out):
    for p in range(PL):
        flat = cells[p].T
        for j in range(LT):
            at = (p * LT + j) * OD
            out[:, at : at + OD, :] = flat[:, j * 128 : (j + 1) * 128].reshape(DOMS, OD, 128)
    turned = jnp.concatenate([(STRETCH * (pot[p] - center) + 3.0 * along[0]).T for p in range(PL)], 0)
    spot = lax.broadcasted_iota(jnp.int32, (NZ, PTS), 1)
    pick = (lax.rem(spot, NZ) == lax.broadcasted_iota(jnp.int32, (NZ, PTS), 0)).astype(jnp.float32)
    wide = jnp.dot(turned, pick, precision=lax.Precision.HIGHEST, preferred_element_type=jnp.float32)
    point = lax.broadcasted_iota(jnp.int32, (NY, PTS), 1)
    first = lax.broadcasted_iota(jnp.int32, (NY, PTS), 0) * NZ
    keep = (point >= first) & (point < first + NZ)
    for p in range(PL):
        row = jnp.sum(jnp.where(keep, wide[p * NY : (p + 1) * NY, :], 0.0), 0, keepdims=True)
        for j in range(LT):
            at = ROWS + p * LT + j
            out[:, at : at + 1, :] = jnp.broadcast_to(row[None, :, j * 128 : (j + 1) * 128], (DOMS, 1, 128))
    out[:, ROWS + POT :, :] = jnp.zeros((DOMS, POT_PAD - POT, 128), jnp.float32)


def filter_kernel(cells, ring, out, one, two, left_a, left_b, prod_a, prod_b):
    group = DOMS // TURNS
    at = [[slice((i * LT + j) * OD, (i * LT + j + 1) * OD) for i in range(PL)] for j in range(LT)]

    def keep(left, s, i, j, pair):
        rows = slice((s * PL + i - 1) * OD, (s * PL + i + 1) * OD)
        hi, lo = split(jnp.concatenate(pair, 0))
        left[rows, j * 128 : (j + 1) * 128] = hi
        left[rows, PTS + j * 128 : PTS + (j + 1) * 128] = lo

    def planes(left, prod, turn):
        rows = slice(turn * group * PL * OD, (turn + 1) * group * PL * OD)
        for n in range(PTS // 256):
            cols = slice(n * 256, (n + 1) * 256)
            prod[rows, cols] = (
                jnp.dot(left[rows, :PTS], ring[:, cols], preferred_element_type=jnp.float32)
                + jnp.dot(left[rows, PTS:], ring[:, cols], preferred_element_type=jnp.float32)
            )

    def across(cur, prior, new, prod, left, back, scale, turn):
        for s in range(turn * group, (turn + 1) * group):
            for j in range(LT):
                line = [cur[b % DOMS, at[j][i], :] for b in (s - 1, s, s + 1) for i in range(PL)]
                fresh = []
                for i in range(PL):
                    mid = PL + i
                    row = (s * PL + i) * OD
                    pot = cells[s, ROWS + i * LT + j, :][None]
                    total = prod[row : row + OD, j * 128 : (j + 1) * 128] + pot * line[mid]
                    for k in range(1, 7):
                        total = total + along[k] * (line[mid + k] + line[mid - k])
                    if prior is not None:
                        total = total - back * prior[s, at[j][i], :]
                    if scale != 1.0:
                        total = total * scale
                    fresh.append(total)
                for i in range(PL):
                    new[s, at[j][i], :] = fresh[i]
                    if left is not None and i % 2:
                        keep(left, s, i, j, fresh[i - 1 : i + 1])

    for turn in range(TURNS):
        for s in range(turn * group, (turn + 1) * group):
            for j in range(LT):
                for i in range(1, PL, 2):
                    keep(left_a, s, i, j, [cells[s, at[j][i - 1], :], cells[s, at[j][i], :]])
        planes(left_a, prod_a, turn)
    values, lefts, prods = [cells, one, two, out], [left_a, left_b, left_a, None], [prod_a, prod_b, prod_a]
    for i, (back, scale) in enumerate(steps()):
        for turn in range(TURNS):
            across(values[i], values[i - 1] if i else None, values[i + 1], prods[i], lefts[i + 1], back, scale, turn)
            if i < DEG - 1:
                planes(lefts[i + 1], prods[i + 1], turn)


def gather_kernel(cells, out):
    for p in range(PL):
        for j in range(LT):
            at = (p * LT + j) * OD
            tile = cells[:, at : at + OD, :].reshape(OB, 128)
            out[p * PTS + j * 128 : p * PTS + (j + 1) * 128, :] = tile.T


def margin_blocks(parts, mine, others, pairs):
    left_hi, left_lo, right_hi, right_lo = parts
    wide = 2 * OB
    nd = NORB // DOMS
    even = lax.rem(lax.axis_index("core"), 2) == 0

    def put(block, i, j):
        for c in range(2):
            for r in range(2):
                first = block[2 * r * nd : (2 * r + 1) * nd, c * OB : (c + 1) * OB]
                second = block[(2 * r + 1) * nd : (2 * r + 2) * nd, c * OB : (c + 1) * OB]
                at = (j // 2, 2 * (j % 2) + c, 2 * (i % 2) + r)
                mine[at] = jnp.where(even, first, second)
                others[at] = jnp.where(even, second, first)

    for i, j in pairs:
        rows, cols = slice(i * wide, (i + 1) * wide), slice(j * wide, (j + 1) * wide)
        block = (
            jnp.dot(left_hi[rows, :], right_hi[:, cols], preferred_element_type=jnp.float32)
            + jnp.dot(left_lo[rows, :], right_hi[:, cols], preferred_element_type=jnp.float32)
            + jnp.dot(left_hi[rows, :], right_lo[:, cols], preferred_element_type=jnp.float32)
        )
        put(block, i, j)
        if i != j:
            put(block.T, j, i)


def far_kernel(cells, flat, mine, others, left_hi, left_lo, right_hi, right_lo, result, done):
    copy = pltpu.make_async_copy(flat, result, done)
    copy.start()
    for b in range(BANDS):
        cols = slice(b * OB, (b + 1) * OB)
        right_hi[:, cols], right_lo[:, cols] = split(cells[b])
        left_hi[cols, :], left_lo[cols, :] = split(cells[b].T)
    margin_blocks((left_hi, left_lo, right_hi, right_lo), mine, others, [(2, 0), (3, 0), (2, 1), (3, 1)])
    copy.wait()


def near_kernel(left_hi, left_lo, right_hi, right_lo, mine, others):
    parts = (left_hi, left_lo, right_hi, right_lo)
    margin_blocks(parts, mine, others, [(0, 0), (1, 0), (1, 1), (2, 2), (3, 2), (3, 3)])


def join_kernel(far, far_other, near, near_other, out):
    for h in range(2):
        here, there = slice(4 * h, 4 * h + 4), slice(4 - 4 * h, 8 - 4 * h)
        out[here, there] = far[h] + far_other[h]
        out[here, here] = near[h] + near_other[h]


def sum_kernel(parts, out):
    total = parts[0]
    for i in range(1, BANDS * DOMS // 2):
        total = total + parts[i]
    out[...] = total * (1.0 / GRID)


def call(kernel, shape, *args, scratch=(), limit=16):
    shapes = shape if isinstance(shape, list) else [shape]
    out = [jax.ShapeDtypeStruct(s, jnp.float32) for s in shapes]
    return pl.pallas_call(
        kernel,
        out_shape=out if isinstance(shape, list) else out[0],
        scratch_shapes=list(scratch),
        compiler_params=pltpu.CompilerParams(vmem_limit_bytes=limit * MIB),
    )(*args)


BAND = ("x", "y_lo")
DOMAIN = ("y_hi", "z", "core")
CHIPS = ("x", "y_lo", "y_hi", "z")


def local(orbitals, potential, ring):
    cells = call(
        spread_kernel,
        (DOMS, ROWS + POT_PAD, 128),
        orbitals.reshape(PL, PTS, OB),
        potential.transpose(0, 2, 1),
    )
    cells = lax.all_to_all(cells, DOMAIN, 0, 0, tiled=True)
    cells = call(
        filter_kernel,
        (DOMS, ROWS, 128),
        cells,
        ring,
        scratch=[pltpu.VMEM((DOMS, ROWS, 128), jnp.float32)] * 2
        + [pltpu.VMEM((NX * OD, 2 * PTS), jnp.bfloat16)] * 2
        + [pltpu.VMEM((NX * OD, PTS), jnp.float32)] * 2,
        limit=32,
    )
    cells = lax.all_to_all(cells, DOMAIN, 0, 0, tiled=True)
    flat = call(gather_kernel, (PL * PTS, OB), cells)
    count = PL * PTS // BANDS
    points = lax.all_to_all(flat.reshape(BANDS, count, OB), BAND, 0, 0, tiled=True)
    shape = (2, BANDS // 2, DOMS // 4, NORB // DOMS, OB)
    half = (jax.ShapeDtypeStruct(shape, jnp.float32),) * 2
    parts = (jax.ShapeDtypeStruct((NORB, count), jnp.bfloat16),) * 2
    parts += (jax.ShapeDtypeStruct((count, NORB), jnp.bfloat16),) * 2
    limits = pltpu.CompilerParams(vmem_limit_bytes=16 * MIB)
    near_by, anywhere = pl.BlockSpec(memory_space=pltpu.VMEM), pl.BlockSpec(memory_space=pl.ANY)
    far, far_other, *parts, result = pl.pallas_call(
        far_kernel,
        out_shape=half + parts + (jax.ShapeDtypeStruct(flat.shape, jnp.float32),),
        in_specs=[near_by, anywhere],
        out_specs=[near_by] * 6 + [anywhere],
        scratch_shapes=[pltpu.SemaphoreType.DMA],
        compiler_params=limits,
    )(points, flat)
    far_other = lax.ppermute(far_other, "core", [(0, 1), (1, 0)])
    near, near_other = pl.pallas_call(near_kernel, out_shape=half, compiler_params=limits)(*parts)
    near_other = lax.ppermute(near_other, "core", [(0, 1), (1, 0)])
    partial = call(join_kernel, (BANDS, DOMS // 2, NORB // DOMS, OB), far, far_other, near, near_other)
    partial = partial.reshape(BANDS * DOMS // 2, NORB // DOMS, OB)
    partial = lax.all_to_all(partial, CHIPS, 0, 0, tiled=True)
    margin = call(sum_kernel, (NORB // DOMS, OB), partial)
    return result.reshape(PL, NY, NZ, OB), margin.T


def solution(mesh):
    mesh = jax.sharding.Mesh(mesh.devices.reshape(4, 2, 2, 4, 2), BAND + DOMAIN)
    grid, pot = P(DOMAIN, None, None, BAND), P(DOMAIN, None, None)
    ring = plane_matrix()
    body = jax.shard_map(
        local,
        mesh=mesh,
        in_specs=(grid, pot, P()),
        out_specs=(grid, P(BAND, DOMAIN)),
        check_vma=False,
    )

    def run(orbitals, potential):
        return body(orbitals, potential, jnp.asarray(ring))

    return run
```

```python
import jax
import jax.numpy as jnp
import numpy as np
from jax import lax
from jax.experimental import pallas as pl
from jax.experimental.pallas import tpu as pltpu
from jax.sharding import PartitionSpec as P

DEG = 3

coeffs = (
    -5369.0 / 1800.0,
    12.0 / 7.0,
    -15.0 / 56.0,
    10.0 / 189.0,
    -1.0 / 112.0,
    2.0 / 1925.0,
    -1.0 / 16632.0,
)
bound_floor = 0.0
bound_cut = 2.0
bound_top = 11.0
center = (bound_top + bound_cut) / 2.0

NX, NY, NZ = 96, 32, 24
PTS = NY * NZ
LT = PTS // 128
BANDS, DOMS = 8, 16
PL = NX // DOMS
NORB = 1024
OB = NORB // BANDS
OD = OB // DOMS
ROWS = PL * LT * OD
POT = PL * LT
POT_PAD = 40
TURNS = 2
GRID = NX * PTS
MIB = 1024 * 1024


STRETCH = 35.0 / 16.0
along = [-0.5 * STRETCH * c for c in coeffs]


def steps():
    half_width = (bound_top - bound_cut) / 2.0
    sigma = half_width / (bound_floor - center)
    gamma = 2.0 / sigma
    scales, backs = [sigma / half_width / STRETCH], [0.0]
    for _ in range(2, DEG + 1):
        second = 1.0 / (gamma - sigma)
        scales.append(2.0 * second / half_width / STRETCH)
        backs.append(sigma * second)
        sigma = second
    out = [(0.0, 1.0)]
    for i in range(1, DEG):
        out.append((backs[i] / (scales[i] * scales[i - 1]), float(np.prod(scales)) if i == DEG - 1 else 1.0))
    return out


def plane_matrix():
    def ring(n):
        m = np.zeros((n, n))
        for k in range(1, 7):
            for i in range(n):
                m[i, (i + k) % n] += along[k]
                m[i, (i - k) % n] += along[k]
        return m

    m = np.asarray(np.kron(ring(NY), np.eye(NZ)) + np.kron(np.eye(NY), ring(NZ)), jnp.bfloat16)
    return np.concatenate([m, m], 0)


def split(value):
    hi = value.astype(jnp.bfloat16)
    return hi, (value - hi.astype(jnp.float32)).astype(jnp.bfloat16)


def spread_kernel(cells, out):
    for p in range(PL):
        flat = cells[p].T
        for j in range(LT):
            at = (p * LT + j) * OD
            out[:, at : at + OD, :] = flat[:, j * 128 : (j + 1) * 128].reshape(DOMS, OD, 128)


def field_kernel(pot, cells, out, rows, done):
    del cells
    turned = jnp.concatenate([(STRETCH * (pot[p] - center) + 3.0 * along[0]).T for p in range(PL)], 0)
    spot = lax.broadcasted_iota(jnp.int32, (NZ, PTS), 1)
    pick = (lax.rem(spot, NZ) == lax.broadcasted_iota(jnp.int32, (NZ, PTS), 0)).astype(jnp.float32)
    wide = jnp.dot(turned, pick, precision=lax.Precision.HIGHEST, preferred_element_type=jnp.float32)
    point = lax.broadcasted_iota(jnp.int32, (NY, PTS), 1)
    first = lax.broadcasted_iota(jnp.int32, (NY, PTS), 0) * NZ
    keep = (point >= first) & (point < first + NZ)
    for p in range(PL):
        row = jnp.sum(jnp.where(keep, wide[p * NY : (p + 1) * NY, :], 0.0), 0, keepdims=True)
        for j in range(LT):
            at = p * LT + j
            rows[:, at : at + 1, :] = jnp.broadcast_to(row[None, :, j * 128 : (j + 1) * 128], (DOMS, 1, 128))
    rows[:, POT:, :] = jnp.zeros((DOMS, POT_PAD - POT, 128), jnp.float32)
    copy = pltpu.make_async_copy(rows, out.at[:, ROWS : ROWS + POT_PAD, :], done)
    copy.start()
    copy.wait()


def filter_kernel(cells, ring, out, one, two, left_a, left_b, prod_a, prod_b):
    group = DOMS // TURNS
    at = [[slice((i * LT + j) * OD, (i * LT + j + 1) * OD) for i in range(PL)] for j in range(LT)]

    def keep(left, s, i, j, pair):
        rows = slice((s * PL + i - 1) * OD, (s * PL + i + 1) * OD)
        hi, lo = split(jnp.concatenate(pair, 0))
        left[rows, j * 128 : (j + 1) * 128] = hi
        left[rows, PTS + j * 128 : PTS + (j + 1) * 128] = lo

    def planes(left, prod, turn):
        rows = slice(turn * group * PL * OD, (turn + 1) * group * PL * OD)
        for n in range(PTS // 256):
            cols = slice(n * 256, (n + 1) * 256)
            prod[rows, cols] = jnp.dot(left[rows, :], ring[:, cols], preferred_element_type=jnp.float32)

    def across(cur, prior, new, prod, left, back, scale, turn):
        for s in range(turn * group, (turn + 1) * group):
            for j in range(LT):
                line = [cur[b % DOMS, at[j][i], :] for b in (s - 1, s, s + 1) for i in range(PL)]
                fresh = []
                for i in range(PL):
                    mid = PL + i
                    row = (s * PL + i) * OD
                    pot = cells[s, ROWS + i * LT + j, :][None]
                    total = prod[row : row + OD, j * 128 : (j + 1) * 128] + pot * line[mid]
                    for k in range(1, 7):
                        total = total + along[k] * (line[mid + k] + line[mid - k])
                    if prior is not None:
                        total = total - back * prior[s, at[j][i], :]
                    if scale != 1.0:
                        total = total * scale
                    fresh.append(total)
                for i in range(PL):
                    new[s, at[j][i], :] = fresh[i]
                    if left is not None and i % 2:
                        keep(left, s, i, j, fresh[i - 1 : i + 1])

    for turn in range(TURNS):
        for s in range(turn * group, (turn + 1) * group):
            for j in range(LT):
                for i in range(1, PL, 2):
                    keep(left_a, s, i, j, [cells[s, at[j][i - 1], :], cells[s, at[j][i], :]])
        planes(left_a, prod_a, turn)
    values, lefts, prods = [cells, one, two, out], [left_a, left_b, left_a, None], [prod_a, prod_b, prod_a]
    for i, (back, scale) in enumerate(steps()):
        for turn in range(TURNS):
            across(values[i], values[i - 1] if i else None, values[i + 1], prods[i], lefts[i + 1], back, scale, turn)
            if i < DEG - 1:
                planes(lefts[i + 1], prods[i + 1], turn)


def gather_kernel(cells, out):
    for p in range(PL):
        for j in range(LT):
            at = (p * LT + j) * OD
            tile = cells[:, at : at + OD, :].reshape(OB, 128)
            out[p * PTS + j * 128 : p * PTS + (j + 1) * 128, :] = tile.T


def margin_blocks(parts, mine, others, pairs):
    left_hi, left_lo, right_hi, right_lo = parts
    wide = 2 * OB
    nd = NORB // DOMS
    even = lax.rem(lax.axis_index("core"), 2) == 0

    def put(block, i, j):
        for c in range(2):
            for r in range(2):
                first = block[2 * r * nd : (2 * r + 1) * nd, c * OB : (c + 1) * OB]
                second = block[(2 * r + 1) * nd : (2 * r + 2) * nd, c * OB : (c + 1) * OB]
                at = (j // 2, 2 * (j % 2) + c, 2 * (i % 2) + r)
                mine[at] = jnp.where(even, first, second)
                others[at] = jnp.where(even, second, first)

    for i, j in pairs:
        rows, cols = slice(i * wide, (i + 1) * wide), slice(j * wide, (j + 1) * wide)
        block = (
            jnp.dot(left_hi[rows, :], right_hi[:, cols], preferred_element_type=jnp.float32)
            + jnp.dot(left_lo[rows, :], right_hi[:, cols], preferred_element_type=jnp.float32)
            + jnp.dot(left_hi[rows, :], right_lo[:, cols], preferred_element_type=jnp.float32)
        )
        put(block, i, j)
        if i != j:
            put(block.T, j, i)


def far_kernel(cells, flat, mine, others, left_hi, left_lo, right_hi, right_lo, result, done):
    copy = pltpu.make_async_copy(flat, result, done)
    copy.start()
    for b in range(BANDS):
        cols = slice(b * OB, (b + 1) * OB)
        right_hi[:, cols], right_lo[:, cols] = split(cells[b])
        left_hi[cols, :], left_lo[cols, :] = split(cells[b].T)
    margin_blocks((left_hi, left_lo, right_hi, right_lo), mine, others, [(2, 0), (3, 0), (2, 1), (3, 1)])
    copy.wait()


def near_kernel(left_hi, left_lo, right_hi, right_lo, mine, others):
    parts = (left_hi, left_lo, right_hi, right_lo)
    margin_blocks(parts, mine, others, [(0, 0), (1, 0), (1, 1), (2, 2), (3, 2), (3, 3)])


def join_kernel(far, far_other, near, near_other, out):
    for h in range(2):
        here, there = slice(4 * h, 4 * h + 4), slice(4 - 4 * h, 8 - 4 * h)
        out[here, there] = far[h] + far_other[h]
        out[here, here] = near[h] + near_other[h]


def sum_kernel(parts, out):
    total = parts[0]
    for i in range(1, BANDS * DOMS // 2):
        total = total + parts[i]
    out[...] = total * (1.0 / GRID)


def call(kernel, shape, *args, scratch=(), limit=16):
    shapes = shape if isinstance(shape, list) else [shape]
    out = [jax.ShapeDtypeStruct(s, jnp.float32) for s in shapes]
    return pl.pallas_call(
        kernel,
        out_shape=out if isinstance(shape, list) else out[0],
        scratch_shapes=list(scratch),
        compiler_params=pltpu.CompilerParams(vmem_limit_bytes=limit * MIB),
    )(*args)


BAND = ("x", "y_lo")
DOMAIN = ("y_hi", "z", "core")
CHIPS = ("x", "y_lo", "y_hi", "z")


def local(orbitals, potential, ring):
    near_by, anywhere = pl.BlockSpec(memory_space=pltpu.VMEM), pl.BlockSpec(memory_space=pl.ANY)
    cells = call(
        spread_kernel,
        (DOMS, ROWS + POT_PAD, 128),
        orbitals.reshape(PL, PTS, OB),
    )
    cells = pl.pallas_call(
        field_kernel,
        out_shape=jax.ShapeDtypeStruct(cells.shape, jnp.float32),
        in_specs=[near_by, anywhere],
        out_specs=anywhere,
        scratch_shapes=[pltpu.VMEM((DOMS, POT_PAD, 128), jnp.float32), pltpu.SemaphoreType.DMA],
        input_output_aliases={1: 0},
        compiler_params=pltpu.CompilerParams(vmem_limit_bytes=16 * MIB),
    )(potential.transpose(0, 2, 1), cells)
    cells = lax.all_to_all(cells, DOMAIN, 0, 0, tiled=True)
    cells = call(
        filter_kernel,
        (DOMS, ROWS, 128),
        cells,
        ring,
        scratch=[pltpu.VMEM((DOMS, ROWS, 128), jnp.float32)] * 2
        + [pltpu.VMEM((NX * OD, 2 * PTS), jnp.bfloat16)] * 2
        + [pltpu.VMEM((NX * OD, PTS), jnp.float32)] * 2,
        limit=32,
    )
    cells = lax.all_to_all(cells, DOMAIN, 0, 0, tiled=True)
    flat = call(gather_kernel, (PL * PTS, OB), cells)
    count = PL * PTS // BANDS
    points = lax.all_to_all(flat.reshape(BANDS, count, OB), BAND, 0, 0, tiled=True)
    shape = (2, BANDS // 2, DOMS // 4, NORB // DOMS, OB)
    half = (jax.ShapeDtypeStruct(shape, jnp.float32),) * 2
    parts = (jax.ShapeDtypeStruct((NORB, count), jnp.bfloat16),) * 2
    parts += (jax.ShapeDtypeStruct((count, NORB), jnp.bfloat16),) * 2
    limits = pltpu.CompilerParams(vmem_limit_bytes=16 * MIB)
    far, far_other, *parts, result = pl.pallas_call(
        far_kernel,
        out_shape=half + parts + (jax.ShapeDtypeStruct(flat.shape, jnp.float32),),
        in_specs=[near_by, anywhere],
        out_specs=[near_by] * 6 + [anywhere],
        scratch_shapes=[pltpu.SemaphoreType.DMA],
        compiler_params=limits,
    )(points, flat)
    far_other = lax.ppermute(far_other, "core", [(0, 1), (1, 0)])
    near, near_other = pl.pallas_call(near_kernel, out_shape=half, compiler_params=limits)(*parts)
    near_other = lax.ppermute(near_other, "core", [(0, 1), (1, 0)])
    partial = call(join_kernel, (BANDS, DOMS // 2, NORB // DOMS, OB), far, far_other, near, near_other)
    partial = partial.reshape(BANDS * DOMS // 2, NORB // DOMS, OB)
    partial = lax.all_to_all(partial, CHIPS, 0, 0, tiled=True)
    margin = call(sum_kernel, (NORB // DOMS, OB), partial)
    return result.reshape(PL, NY, NZ, OB), margin.T


def solution(mesh):
    mesh = jax.sharding.Mesh(mesh.devices.reshape(4, 2, 2, 4, 2), BAND + DOMAIN)
    grid, pot = P(DOMAIN, None, None, BAND), P(DOMAIN, None, None)
    ring = plane_matrix()
    body = jax.shard_map(
        local,
        mesh=mesh,
        in_specs=(grid, pot, P()),
        out_specs=(grid, P(BAND, DOMAIN)),
        check_vma=False,
    )

    def run(orbitals, potential):
        return body(orbitals, potential, jnp.asarray(ring))

    return run
```
